512 devices in a mesh: section: 8 (over x, z_hi), seq: 32 (over z_lo, y), cfg: 2 (over core).
Axes of the slice: x: 4, y: 8, z: 8 (z_hi: 2, z_lo: 4; z = z_hi * 4 + z_lo), core: 2. Of those that a mesh axis runs over, the one named last changes fastest.
Arguments:
- hidden: bfloat16 [2, 8, 1024, 2048], P('cfg', 'section', 'seq'), may hold values from -6 to 6
- queries: bfloat16 [2, 8, 1024, 2048], P('cfg', 'section', 'seq')
- fresh_keys: bfloat16 [2, 8, 1024, 2048], P('cfg', 'section', 'seq'), may hold values from -6 to 6
- fresh_values: bfloat16 [2, 8, 1024, 2048], P('cfg', 'section', 'seq'), may hold values from -6 to 6
- stale_keys: bfloat16 [2, 8, 32, 4224, 128], P('cfg', 'section', 'seq')
- stale_values: bfloat16 [2, 8, 32, 4224, 128], P('cfg', 'section', 'seq'), may hold values from -6 to 6
- gate_table: float32 [50, 8, 2048], P(None, 'section'), may hold values from -6 to 6
- timestep: int32 [], replicated, may hold values from 0 to 49
- patch_index: int32 [], replicated, may hold values from 0 to 7
- text_lengths: int32 [2], P('cfg'), may hold values from 32 to 256, as said below
Outputs:
- handed: bfloat16 [2, 8, 1024, 2048], P('cfg', 'section', 'seq')
The draws below stay inside these ranges and needn't reach their ends.
Inputs may be any that keep to these rules, and one draw needn't show every extreme that they name: `text_lengths`: one of the two branches has all 256 text tokens live.
All inputs are finite; a program needn't handle non-finite values.
Results may differ from the reference program's by a relative error of at most 0.0075.
Values may be sent and summed in bfloat16 or wider, within the bound.
A program may use at most 64 MiB of HBM per device.

```python
import jax
import jax.numpy as jnp
from jax import lax

HEADS = 16
HEAD_DIM = 128
PATCHES = 8
TXT = 256
STEPS = 50
PATCH_DEV = 32
FEAT = 2048
PATCH = 1024
VIDEO = 8192
HALF_KEYS = 4224
N_SECTION = 8
N_SEQ = 32


def draw_queries(key, part):
    key = jax.random.fold_in(key, 11)
    shape = (2, N_SECTION, PATCH, HEADS, HEAD_DIM)
    base = 2.0 * jax.random.normal(key, shape, jnp.float32)
    return base.reshape(2, N_SECTION, PATCH, FEAT).astype(jnp.bfloat16)


def draw_stale_keys(key, part):
    key = jax.random.fold_in(key, 12)
    shape = (2, N_SECTION, 2 * HEADS, HALF_KEYS, HEAD_DIM)
    base = jax.random.normal(key, shape, jnp.float32)
    return base.astype(jnp.bfloat16)


def draw_text_lengths(key, part):
    key = jax.random.fold_in(key, 13)
    first_key, second_key = jax.random.split(key)
    drawn = jax.random.randint(first_key, (2,), TXT // 8, TXT + 1)
    full_branch = jax.random.randint(second_key, (), 0, 2)
    return jnp.where(jnp.arange(2) == full_branch, TXT, drawn).astype(jnp.int32)


def level_of(stream_key, dims, cuts, least, top_value):
    gain = 1.0
    for dim, blocks in cuts:
        heights = jax.random.uniform(jax.random.fold_in(jax.random.fold_in(stream_key, 6), dim), (blocks,), jnp.float32, least / len(cuts), top_value / len(cuts))
        gain = gain * jnp.repeat(jnp.exp(heights), dims[dim] // blocks).reshape((-1,) + (1,) * (len(dims) - 1 - dim))
    return gain


def centred(rng, dims, width, reach, cuts=(), kind=jnp.bfloat16):
    gain = level_of(rng, dims, cuts, -0.22, 0.18) if cuts else 1.0
    array = jax.random.normal(rng, dims, jnp.float32) * width * gain
    return jnp.minimum(jnp.maximum(array, -reach), reach).astype(kind)


def setup_inputs(seed: int = 0) -> dict:
    key_list = jax.random.split(jax.random.key(seed), 11)
    hidden = centred(key_list[0], (2, N_SECTION, PATCH, FEAT), 1.0, 6.0, ((0, 2), (1, 8), (2, 32)))
    queries = draw_queries(jax.random.fold_in(key_list[10], 71), 0)
    fresh_keys = centred(key_list[2], (2, N_SECTION, PATCH, FEAT), 1.0, 6.0, ((0, 2), (1, 8), (2, 32)))
    fresh_values = centred(key_list[3], (2, N_SECTION, PATCH, FEAT), 1.0, 6.0, ((0, 2), (1, 8), (2, 32)))
    stale_keys = draw_stale_keys(jax.random.fold_in(key_list[10], 71), 0)
    stale_values = centred(key_list[5], (2, N_SECTION, 2 * HEADS, HALF_KEYS, HEAD_DIM), 1.0, 6.0, ((0, 2), (1, 8), (2, 32)))
    gate_table = centred(key_list[6], (STEPS, N_SECTION, FEAT), 1.5, 6.0, ((1, 8),), jnp.float32)
    timestep = jax.random.randint(key_list[7], (), 0, STEPS).astype(jnp.int32)
    patch_index = jax.random.randint(key_list[8], (), 0, PATCHES).astype(jnp.int32)
    text_lengths = draw_text_lengths(jax.random.fold_in(key_list[10], 71), 0)
    return {"hidden": hidden, "queries": queries, "fresh_keys": fresh_keys, "fresh_values": fresh_values, "stale_keys": stale_keys, "stale_values": stale_values, "gate_table": gate_table, "timestep": timestep, "patch_index": patch_index, "text_lengths": text_lengths}


GUIDE = 5.0


def half_attention(query_rows, key_rows, value_rows, live, scale):
    scores = jnp.dot(query_rows, key_rows.T, preferred_element_type=jnp.float32) * scale
    masked = jnp.where(live[None, :], scores, -jnp.inf)
    highest = jnp.max(masked, axis=1)
    exps = jnp.exp(masked - highest[:, None])
    totals = jnp.sum(exps, axis=1)
    summed = jnp.dot(exps.astype(jnp.bfloat16), value_rows, preferred_element_type=jnp.float32)
    partial_value = (summed / totals[:, None]).astype(jnp.bfloat16)
    return partial_value, highest + jnp.log(totals)


def reference(hidden, queries, fresh_keys, fresh_values, stale_keys, stale_values, gate_table, timestep, patch_index, text_lengths):
    scale = HEAD_DIM ** -0.5
    gates = lax.dynamic_index_in_dim(gate_table, timestep, 0, keepdims=False)
    positions = jnp.arange(2 * HALF_KEYS, dtype=jnp.int32)
    fresh_live = jnp.ones((PATCH // 2,), dtype=jnp.bool_)
    section_outs = []
    for branch in range(2):
        branch_outs = []
        for section in range(N_SECTION):
            patch_start = (jnp.mod(patch_index - section, PATCHES) * PATCH).astype(jnp.int32)
            outside = (positions < patch_start) | (positions >= patch_start + PATCH)
            text_live = (positions >= VIDEO) & (positions - VIDEO < text_lengths[branch])
            live_stale = (((positions < VIDEO) & outside) | text_live).reshape(2, HALF_KEYS)
            stale_k = stale_keys[branch, section].reshape(HEADS, 2, HALF_KEYS, HEAD_DIM)
            stale_v = stale_values[branch, section].reshape(HEADS, 2, HALF_KEYS, HEAD_DIM)
            new_k = jnp.transpose(fresh_keys[branch, section].reshape(N_SEQ, 2, PATCH_DEV // 2, HEADS, HEAD_DIM), (3, 1, 0, 2, 4)).reshape(HEADS, 2, PATCH // 2, HEAD_DIM)
            new_v = jnp.transpose(fresh_values[branch, section].reshape(N_SEQ, 2, PATCH_DEV // 2, HEADS, HEAD_DIM), (3, 1, 0, 2, 4)).reshape(HEADS, 2, PATCH // 2, HEAD_DIM)
            query_heads = jnp.transpose(queries[branch, section].reshape(PATCH, HEADS, HEAD_DIM), (1, 0, 2))

            def one_head(operands, live_stale=live_stale):
                query_rows, keys_s, values_s, keys_n, values_n = operands
                parts = []
                lses = []
                for half in range(2):
                    live = jnp.concatenate([live_stale[half], fresh_live])
                    keys_all = jnp.concatenate([keys_s[half], keys_n[half]], axis=0)
                    values_all = jnp.concatenate([values_s[half], values_n[half]], axis=0)
                    part, lse = half_attention(query_rows, keys_all, values_all, live, scale)
                    parts.append(part.astype(jnp.float32))
                    lses.append(lse)
                joint = jnp.maximum(lses[0], lses[1])
                first = jnp.exp(lses[0] - joint)
                second = jnp.exp(lses[1] - joint)
                merged = (first[:, None] * parts[0] + second[:, None] * parts[1]) / (first + second)[:, None]
                return merged.astype(jnp.bfloat16)

            attended = lax.map(one_head, (query_heads, stale_k, stale_v, new_k, new_v))
            attended = jnp.transpose(attended, (1, 0, 2)).reshape(PATCH, FEAT)
            section_out = (hidden[branch, section].astype(jnp.float32) + gates[section] * attended.astype(jnp.float32)).astype(jnp.bfloat16)
            branch_outs.append(section_out)
        section_outs.append(branch_outs)
    guided_side = section_outs[0][N_SECTION - 1].astype(jnp.float32)
    plain_side = section_outs[1][N_SECTION - 1].astype(jnp.float32)
    guided = (plain_side + GUIDE * (guided_side - plain_side)).astype(jnp.bfloat16)
    handed = []
    for branch in range(2):
        handed.append(jnp.stack([guided] + section_outs[branch][:N_SECTION - 1], axis=0))
    return jnp.stack(handed, axis=0)
```

```python
import functools
import math

import jax
import jax.numpy as jnp
from jax import lax
from jax.experimental import pallas as pl
from jax.experimental.pallas import tpu as pltpu
from jax.sharding import PartitionSpec as P

HEADS = 16
DIM = 128
PATCHES = 8
PATCH = 1024
VIDEO = 8192
GUIDE = 5.0
MESH = pl.DeviceIdType.MESH

N_SEQ = 32
N_SECTION = 8
TOKENS = 32
HALF = 16
STALE = 4224
FRESH = 512
KEYS = STALE + FRESH
CHUNK = 512
N_CHUNK = PATCH // CHUNK
BLOCKS = CHUNK // TOKENS
STALE_BLOCKS = (1024, 1024, 1024, 1152)
LOG2E = math.log2(math.e)
RATE = DIM**-0.5 * LOG2E


def peer_of(z, y, k):
    j = lax.rem(k, 8)
    step = lax.div(j + 1, 2)
    offset = jnp.where(lax.rem(j, 2) == 1, step, 8 - step)
    other = lax.rem(y + offset, 8)
    plane = lax.bitwise_xor(z, lax.div(k, 8))
    return plane * 8 + other


def kernel(
    patch_ref,
    text_ref,
    time_ref,
    hidden_hbm,
    q_hbm,
    k_hbm,
    v_hbm,
    sk_hbm,
    sv_hbm,
    gate_hbm,
    out_ref,
    q_in,
    k_in,
    v_in,
    h_in,
    q_out,
    kv_out,
    hid_out,
    q_all,
    kv_land,
    hid_land,
    keys,
    vals,
    gates,
    high,
    acc,
    part,
    lse_s,
    lse_out,
    part_land,
    lse_land,
    fin,
    core_out,
    core_land,
    in_sem,
    stale_sem,
    q_send,
    q_recv,
    kv_send,
    kv_recv,
    hid_send,
    hid_recv,
    part_send,
    part_recv,
    lse_send,
    lse_recv,
    core_send,
    core_recv,
    fin_send,
    fin_recv,
    okay,
):
    section = lax.axis_index("section")
    seq = lax.axis_index("seq")
    core = lax.axis_index("cfg")
    z = lax.div(seq, 8)
    y = lax.rem(seq, 8)
    head = lax.div(seq, 2)
    side = lax.rem(seq, 2)
    partner = lax.bitwise_xor(seq, 1)
    following = lax.rem(section + 1, N_SECTION)
    previous = lax.rem(section + N_SECTION - 1, N_SECTION)
    last = section == N_SECTION - 1
    head_cols = pl.ds(pl.multiple_of(head * DIM, DIM), DIM)

    barrier = pltpu.get_barrier_semaphore()

    def greet(k, carry):
        pl.semaphore_signal(
            barrier, inc=1, device_id={"seq": peer_of(z, y, k)}, device_id_type=MESH
        )
        return carry

    lax.fori_loop(1, N_SEQ, greet, 0)
    pl.semaphore_signal(barrier, inc=1, device_id={"section": following}, device_id_type=MESH)

    @pl.when(last)
    def _():
        pl.semaphore_signal(barrier, inc=1, device_id={"cfg": 1 - core}, device_id_type=MESH)

    loads = [
        pltpu.make_async_copy(src, dst, in_sem.at[i])
        for i, (src, dst) in enumerate(
            [
                (q_hbm, q_in),
                (k_hbm, k_in),
                (v_hbm, v_in),
                (hidden_hbm, h_in),
                (gate_hbm.at[:, 0, head_cols], gates),
            ]
        )
    ]
    for load in loads:
        load.start()
    stale_k = pltpu.make_async_copy(sk_hbm, keys.at[pl.ds(0, STALE)], stale_sem.at[0])
    stale_v = pltpu.make_async_copy(
        sv_hbm, vals.at[pl.ds(0, STALE), pl.ds(0, DIM)], stale_sem.at[1]
    )
    stale_k.start()
    stale_v.start()

    loads[0].wait()
    for h in range(HEADS):
        q_out[h] = q_in[:, h * DIM : (h + 1) * DIM]
    loads[1].wait()
    loads[2].wait()
    for h in range(HEADS):
        for r in range(2):
            rows = slice(r * HALF, (r + 1) * HALF)
            cols = slice(h * DIM, (h + 1) * DIM)
            kv_out[2 * h + r, 0] = k_in[rows, cols]
            kv_out[2 * h + r, 1] = v_in[rows, cols]
    loads[3].wait()
    for h in range(HEADS):
        for r in range(2):
            rows = slice(r * HALF, (r + 1) * HALF)
            cols = slice(h * DIM, (h + 1) * DIM)
            hid_out[2 * h + r] = h_in[rows, cols]

    pl.semaphore_wait(barrier, N_SEQ + jnp.where(last, 1, 0))
    pl.semaphore_signal(okay, inc=1, device_id={"section": previous}, device_id_type=MESH)

    mine = pl.ds(pl.multiple_of(seq * TOKENS, TOKENS), TOKENS)
    own_q = pltpu.make_async_copy(q_out.at[head], q_all.at[mine], q_recv.at[z])
    own_kv = pltpu.make_async_copy(kv_out.at[seq], kv_land.at[seq], kv_recv)
    own_hid = pltpu.make_async_copy(hid_out.at[seq], hid_land.at[seq], hid_recv)

    def send_q(k, carry):
        p = peer_of(z, y, k)
        pltpu.make_async_remote_copy(
            src_ref=q_out.at[lax.div(p, 2)],
            dst_ref=q_all.at[mine],
            send_sem=q_send,
            recv_sem=q_recv.at[z],
            device_id={"seq": p},
            device_id_type=MESH,
        ).start()
        return carry

    def send_kv(k, carry):
        p = peer_of(z, y, k)
        pltpu.make_async_remote_copy(
            src_ref=kv_out.at[p],
            dst_ref=kv_land.at[seq],
            send_sem=kv_send,
            recv_sem=kv_recv,
            device_id={"seq": p},
            device_id_type=MESH,
        ).start()
        return carry

    def send_hid(k, carry):
        p = peer_of(z, y, k)
        pltpu.make_async_remote_copy(
            src_ref=hid_out.at[p],
            dst_ref=hid_land.at[seq],
            send_sem=hid_send,
            recv_sem=hid_recv,
            device_id={"seq": p},
            device_id_type=MESH,
        ).start()
        return carry

    own_q.start()
    own_kv.start()
    own_hid.start()
    lax.fori_loop(1, N_SEQ, send_q, 0)
    lax.fori_loop(1, N_SEQ, send_kv, 0)
    lax.fori_loop(1, N_SEQ, send_hid, 0)

    patch_start = lax.rem(patch_ref[0] - section + PATCHES, PATCHES) * PATCH
    text_live = text_ref[0]
    first = side * STALE
    stale_k.wait()
    stale_v.wait()
    dead_first = jnp.logical_and(first >= patch_start, first < patch_start + PATCH)
    use_far = jnp.where(dead_first, 1.0, 0.0).astype(jnp.float32)
    spare = (
        keys[0:16, :].astype(jnp.float32)[0:1] * (1.0 - use_far)
        + keys[2048:2064, :].astype(jnp.float32)[0:1] * use_far
    )

    def mask_rows(i, carry):
        rows = pl.ds(pl.multiple_of(i * 128, 128), 128)
        position = first + i * 128 + lax.broadcasted_iota(jnp.int32, (128, DIM), 0)
        outside = jnp.logical_or(position < patch_start, position >= patch_start + PATCH)
        video = jnp.logical_and(position < VIDEO, outside)
        text = jnp.logical_and(position >= VIDEO, position - VIDEO < text_live)
        live = jnp.logical_or(video, text)
        key_rows = keys[rows, :].astype(jnp.float32)
        keys[rows, :] = jnp.where(live, key_rows, spare).astype(jnp.bfloat16)
        value_rows = vals[rows, 0:DIM].astype(jnp.float32)
        vals[rows, 0:DIM] = jnp.where(live, value_rows, 0.0).astype(jnp.bfloat16)
        vals[rows, DIM : 2 * DIM] = jnp.where(live, 1.0, 0.0).astype(jnp.bfloat16)
        return carry

    lax.fori_loop(0, STALE // 128, mask_rows, 0)
    vals[STALE:KEYS, DIM : 2 * DIM] = jnp.ones((FRESH, DIM), jnp.bfloat16)

    def attend(q, start, count, top, total):
        scores = lax.dot_general(
            q,
            keys[start : start + count, :],
            (((1,), (1,)), ((), ())),
            preferred_element_type=jnp.float32,
        )
        block_top = jnp.max(scores, axis=1, keepdims=True)
        new_top = block_top if top is None else jnp.maximum(top, block_top)
        weights = jnp.exp2((scores - new_top) * RATE).astype(jnp.bfloat16)
        summed = jnp.dot(
            weights, vals[start : start + count, :], preferred_element_type=jnp.float32
        )
        if top is not None:
            summed = total * jnp.exp2((top - new_top) * RATE) + summed
        return new_top, summed

    half_rows = CHUNK // 2

    def chunk_at(i):
        return lax.bitwise_xor(lax.div(z, 2), i)

    def stale_pass(i, carry):
        c = chunk_at(i)
        rows = pl.ds(pl.multiple_of(c * CHUNK, CHUNK), CHUNK)
        for g in range(2):
            plane = 2 * c + g
            plane_rows = q_all.at[pl.ds(pl.multiple_of(plane * 256, 256), 256)]
            pltpu.make_async_copy(plane_rows, plane_rows, q_recv.at[plane]).wait()
        q = q_all[rows, :]
        top, total, start = None, None, 0
        for count in STALE_BLOCKS:
            top, total = attend(q, start, count, top, total)
            start += count
        high[rows, :] = top
        acc[rows, :] = total
        return carry

    lax.fori_loop(0, N_CHUNK, stale_pass, 0)

    pltpu.make_async_copy(kv_land, kv_land, kv_recv).wait()
    keys[STALE:KEYS, :] = kv_land[:, 0].reshape(FRESH, DIM)
    vals[STALE:KEYS, 0:DIM] = kv_land[:, 1].reshape(FRESH, DIM)

    def part_copy(c):
        blocks = pl.ds(pl.multiple_of(c * BLOCKS, BLOCKS), BLOCKS)
        return pltpu.make_async_remote_copy(
            src_ref=part.at[blocks, 1 - side],
            dst_ref=part_land.at[blocks],
            send_sem=part_send.at[c],
            recv_sem=part_recv.at[c],
            device_id={"seq": partner},
            device_id_type=MESH,
        )

    def lse_copy(c):
        return pltpu.make_async_remote_copy(
            src_ref=lse_out.at[c],
            dst_ref=lse_land.at[c],
            send_sem=lse_send.at[c],
            recv_sem=lse_recv.at[c],
            device_id={"seq": partner},
            device_id_type=MESH,
        )

    def fresh_pass(i, carry):
        c = chunk_at(i)
        rows = pl.ds(pl.multiple_of(c * CHUNK, CHUNK), CHUNK)
        blocks = pl.ds(pl.multiple_of(c * BLOCKS, BLOCKS), BLOCKS)
        top, total = attend(q_all[rows, :], STALE, FRESH, high[rows, :], acc[rows, :])
        weight = total[:, DIM : 2 * DIM]
        partial = (total[:, 0:DIM] / weight).astype(jnp.bfloat16)
        part[blocks] = partial.reshape(BLOCKS, 2, HALF, DIM)
        part_copy(c).start()
        lse = top * RATE + jnp.log2(weight)
        lse_s[blocks] = lse.reshape(BLOCKS, 2, HALF, DIM)
        away = lse_s[blocks, 1 - side].reshape(half_rows, DIM)
        lse_out[c] = jnp.transpose(away)[0:8, :]
        lse_copy(c).start()
        return carry

    lax.fori_loop(0, N_CHUNK, fresh_pass, 0)

    loads[4].wait()
    gate = gates[pl.ds(time_ref[0], 1), :]
    pltpu.make_async_copy(hid_land, hid_land, hid_recv).wait()
    pl.semaphore_wait(okay, 1)

    def core_copy(c):
        blocks = pl.ds(pl.multiple_of(c * BLOCKS, BLOCKS), BLOCKS)
        return pltpu.make_async_remote_copy(
            src_ref=core_out.at[blocks],
            dst_ref=core_land.at[blocks],
            send_sem=core_send.at[c],
            recv_sem=core_recv.at[c],
            device_id={"cfg": 1 - core},
            device_id_type=MESH,
        )

    def send_fin(c):
        def send_block(b, carry):
            token_device = c * BLOCKS + b
            pltpu.make_async_remote_copy(
                src_ref=fin.at[token_device],
                dst_ref=out_ref.at[pl.ds(pl.multiple_of(side * HALF, HALF), HALF), head_cols],
                send_sem=fin_send,
                recv_sem=fin_recv,
                device_id={"section": following, "seq": token_device},
                device_id_type=MESH,
            ).start()
            return carry

        lax.fori_loop(0, BLOCKS, send_block, 0)

    def combine_pass(i, carry):
        c = chunk_at(i)
        blocks = pl.ds(pl.multiple_of(c * BLOCKS, BLOCKS), BLOCKS)
        lse_copy(c).wait_recv()
        part_copy(c).wait_recv()
        own_lse = lse_s[blocks, side].reshape(half_rows, DIM)
        other_lse = jnp.transpose(jnp.broadcast_to(lse_land[c, 0:1, :], (DIM, half_rows)))
        joint = jnp.maximum(own_lse, other_lse)
        own_weight = jnp.exp2(own_lse - joint)
        other_weight = jnp.exp2(other_lse - joint)
        own_part = part[blocks, side].reshape(half_rows, DIM).astype(jnp.float32)
        other_part = part_land[blocks].reshape(half_rows, DIM).astype(jnp.float32)
        merged = (own_part * own_weight + other_part * other_weight) / (own_weight + other_weight)
        attended = merged.astype(jnp.bfloat16).astype(jnp.float32)
        held = hid_land[blocks].reshape(half_rows, DIM).astype(jnp.float32)
        result = (held + gate * attended).astype(jnp.bfloat16).reshape(BLOCKS, HALF, DIM)

        @pl.when(last)
        def _():
            core_out[blocks] = result
            core_copy(c).start()

        @pl.when(jnp.logical_not(last))
        def _():
            fin[blocks] = result
            send_fin(c)

        return carry

    lax.fori_loop(0, N_CHUNK, combine_pass, 0)

    @pl.when(last)
    def _():
        def guide_pass(i, carry):
            c = chunk_at(i)
            blocks = pl.ds(pl.multiple_of(c * BLOCKS, BLOCKS), BLOCKS)
            core_copy(c).wait_recv()
            here = core_out[blocks].astype(jnp.float32)
            there = core_land[blocks].astype(jnp.float32)
            is_first = jnp.where(core == 0, 1.0, 0.0).astype(jnp.float32)
            guided_side = here * is_first + there * (1.0 - is_first)
            plain_side = there * is_first + here * (1.0 - is_first)
            fin[blocks] = (plain_side + GUIDE * (guided_side - plain_side)).astype(jnp.bfloat16)
            send_fin(c)
            core_copy(c).wait_send()
            return carry

        lax.fori_loop(0, N_CHUNK, guide_pass, 0)

    def drain(i, carry):
        part_copy(i).wait_send()
        lse_copy(i).wait_send()
        return carry

    lax.fori_loop(0, N_CHUNK, drain, 0)

    def sent(ref, sem):
        pltpu.make_async_copy(ref, ref, sem).wait()

    for _ in range(2):
        sent(q_out.at[pl.ds(0, 15)], q_send)
    sent(q_out.at[0], q_send)
    sent(kv_out.at[pl.ds(0, N_SEQ - 1)], kv_send)
    sent(hid_out.at[pl.ds(0, N_SEQ - 1)], hid_send)
    sent(fin, fin_send)
    pltpu.make_async_copy(fin, fin, fin_recv).wait()


def body(
    hidden, queries, fresh_keys, fresh_values, stale_keys, stale_values, gate_table, timestep,
    patch_index, text_lengths,
):
    bf16, f32 = jnp.bfloat16, jnp.float32
    flat = (TOKENS, HEADS * DIM)
    dma, regular = pltpu.SemaphoreType.DMA, pltpu.SemaphoreType.REGULAR
    scratch = [
        pltpu.VMEM(flat, bf16),
        pltpu.VMEM(flat, bf16),
        pltpu.VMEM(flat, bf16),
        pltpu.VMEM(flat, bf16),
        pltpu.VMEM((HEADS, TOKENS, DIM), bf16),
        pltpu.VMEM((N_SEQ, 2, HALF, DIM), bf16),
        pltpu.VMEM((N_SEQ, HALF, DIM), bf16),
        pltpu.VMEM((PATCH, DIM), bf16),
        pltpu.VMEM((N_SEQ, 2, HALF, DIM), bf16),
        pltpu.VMEM((N_SEQ, HALF, DIM), bf16),
        pltpu.VMEM((KEYS, DIM), bf16),
        pltpu.VMEM((KEYS, 2 * DIM), bf16),
        pltpu.VMEM((50, DIM), f32),
        pltpu.VMEM((PATCH, 1), f32),
        pltpu.VMEM((PATCH, 2 * DIM), f32),
        pltpu.VMEM((N_SEQ, 2, HALF, DIM), bf16),
        pltpu.VMEM((N_SEQ, 2, HALF, DIM), f32),
        pltpu.VMEM((N_CHUNK, 8, CHUNK // 2), f32),
        pltpu.VMEM((N_SEQ, HALF, DIM), bf16),
        pltpu.VMEM((N_CHUNK, 8, CHUNK // 2), f32),
        pltpu.VMEM((N_SEQ, HALF, DIM), bf16),
        pltpu.VMEM((N_SEQ, HALF, DIM), bf16),
        pltpu.VMEM((N_SEQ, HALF, DIM), bf16),
        dma((5,)),
        dma((2,)),
        dma,
        dma((4,)),
        dma,
        dma,
        dma,
        dma,
        dma((N_CHUNK,)),
        dma((N_CHUNK,)),
        dma((N_CHUNK,)),
        dma((N_CHUNK,)),
        dma((N_CHUNK,)),
        dma((N_CHUNK,)),
        dma,
        dma,
        regular,
    ]
    smem = pl.BlockSpec(memory_space=pltpu.SMEM)
    anywhere = pl.BlockSpec(memory_space=pl.ANY)
    out = pl.pallas_call(
        kernel,
        out_shape=jax.ShapeDtypeStruct(flat, bf16),
        in_specs=[smem] * 3 + [anywhere] * 7,
        out_specs=anywhere,
        scratch_shapes=scratch,
        compiler_params=pltpu.CompilerParams(
            collective_id=0, has_side_effects=True, vmem_limit_bytes=56 * 2**20
        ),
        cost_estimate=pl.CostEstimate(
            flops=4 * PATCH * KEYS * DIM, bytes_accessed=2**22, transcendentals=PATCH * KEYS
        ),
    )(
        patch_index.reshape(1),
        text_lengths,
        timestep.reshape(1),
        hidden.reshape(flat),
        queries.reshape(flat),
        fresh_keys.reshape(flat),
        fresh_values.reshape(flat),
        stale_keys.reshape(STALE, DIM),
        stale_values.reshape(STALE, DIM),
        gate_table,
    )
    return out.reshape(1, 1, TOKENS, HEADS * DIM)


def solution(mesh):
    rows = P("cfg", "section", "seq", None)
    stale = P("cfg", "section", "seq", None, None)
    return jax.shard_map(
        body,
        mesh=mesh,
        in_specs=(
            rows, rows, rows, rows, stale, stale, P(None, "section", None), P(), P(), P("cfg"),
        ),
        out_specs=rows,
        check_vma=False,
    )
```

```python
import functools
import math

import jax
import jax.numpy as jnp
from jax import lax
from jax.experimental import pallas as pl
from jax.experimental.pallas import tpu as pltpu
from jax.sharding import PartitionSpec as P

HEADS = 16
DIM = 128
PATCHES = 8
PATCH = 1024
VIDEO = 8192
GUIDE = 5.0
MESH = pl.DeviceIdType.MESH

N_SECTION = 8
TOKENS = 32
STALE = 4224
FRESH = 512
KEYS = STALE + FRESH
PLANES = 4
NEAR = 4
PLANE_ROWS = NEAR * TOKENS
ROWS = 2 * PLANE_ROWS
SIDE_ROWS = PLANES * PLANE_ROWS
STALE_PARTS = ((0, 1024), (1024, 1024), (2048, 1024), (3072, 1152))
FRESH_PART = (STALE, FRESH)
LOG2E = math.log2(math.e)
RATE = DIM**-0.5 * LOG2E


def kernel(
    patch_hbm,
    text_hbm,
    time_hbm,
    hidden_hbm,
    q_hbm,
    k_hbm,
    v_hbm,
    sk_hbm,
    sv_hbm,
    gate_hbm,
    out_ref,
    q_in,
    k_in,
    v_in,
    h_in,
    kv_out,
    q_all,
    kv_land,
    hid_land,
    keys,
    vals,
    gates,
    high,
    acc,
    part_out,
    part_own,
    part_land,
    lse_own,
    lse_out,
    lse_land,
    fin,
    core_out,
    core_land,
    patch_ref,
    text_ref,
    time_ref,
    in_sem,
    stale_sem,
    q_send,
    q_recv,
    pass_send,
    pass_recv,
    kv_send,
    kv_recv,
    hid_send,
    hid_recv,
    part_send,
    part_recv,
    lse_send,
    lse_recv,
    core_send,
    core_recv,
    fin_send,
    fin_recv,
    above,
    okay,
):
    section = lax.axis_index("section")
    seq = lax.axis_index("seq")
    core = lax.axis_index("cfg")
    z = seq >> 3
    y = seq & 7
    head = seq >> 1
    side = seq & 1
    partner = seq ^ 1
    following = (section + 1) & 7
    previous = (section + 7) & 7
    odd = (section & 1) == 1
    last = section == N_SECTION - 1

    def cols_of(h):
        return pl.ds(pl.multiple_of(h * DIM, DIM), DIM)

    barrier = pltpu.get_barrier_semaphore()
    for step in (4, 3, 5, 2, 6, 1, 7):
        pl.semaphore_signal(
            barrier, inc=1, device_id={"seq": (z << 3) | ((y + step) & 7)}, device_id_type=MESH
        )

    @pl.when(jnp.logical_not(odd))
    def _():
        for other in (following, previous):
            pl.semaphore_signal(
                barrier, inc=1, device_id={"section": other}, device_id_type=MESH
            )

    @pl.when(last)
    def _():
        pl.semaphore_signal(barrier, inc=1, device_id={"cfg": 1 - core}, device_id_type=MESH)

    loads = [
        pltpu.make_async_copy(src, dst, in_sem.at[i])
        for i, (src, dst) in enumerate(
            [
                (q_hbm, q_in),
                (k_hbm, k_in),
                (v_hbm, v_in),
                (hidden_hbm, h_in),
                (gate_hbm.at[:, 0, cols_of(head)], gates),
                (patch_hbm, patch_ref),
                (text_hbm, text_ref),
                (time_hbm, time_ref),
            ]
        )
    ]
    for load in loads:
        load.start()
    stale_k = pltpu.make_async_copy(sk_hbm, keys.at[pl.ds(0, STALE)], stale_sem.at[0])
    stale_v = pltpu.make_async_copy(
        sv_hbm, vals.at[pl.ds(0, STALE), pl.ds(0, DIM)], stale_sem.at[1]
    )
    stale_k.start()
    stale_v.start()
    for load in loads[:3]:
        load.wait()
    for h in range(HEADS):
        kv_out[h, 0] = k_in[:, h * DIM : (h + 1) * DIM]
        kv_out[h, 1] = v_in[:, h * DIM : (h + 1) * DIM]
    loads[3].wait()

    def slot_of(pair):
        return (y - pair + 3) & 7

    def nearest(plane, turn):
        pair = (plane << 3) | ((y + 2 * turn) & 6)
        slot = slot_of(pair)
        return pair | (slot >> 2), pair >> 1, slot

    def q_rows(slot):
        start = (slot >> 2) * SIDE_ROWS + z * PLANE_ROWS + (slot & 3) * TOKENS
        return pl.ds(pl.multiple_of(start, TOKENS), TOKENS)

    def block_of(slot):
        return z * NEAR + (slot & 3)

    mine = slot_of(seq & 30)
    own_q = pltpu.make_async_copy(
        q_in.at[:, cols_of(head)], q_all.at[q_rows(mine)], q_recv.at[z >> 1]
    )
    own_kv = pltpu.make_async_copy(kv_out.at[head], kv_land.at[block_of(mine)], kv_recv)
    own_hid = pltpu.make_async_copy(
        h_in.at[:, cols_of(head)], hid_land.at[block_of(mine)], hid_recv
    )
    own_q.start()
    own_kv.start()
    own_hid.start()

    def send_q(plane, turn):
        target, h, slot = nearest(plane, turn)
        pltpu.make_async_remote_copy(
            src_ref=q_in.at[:, cols_of(h)],
            dst_ref=q_all.at[q_rows(slot)],
            send_sem=q_send,
            recv_sem=q_recv.at[z >> 1],
            device_id={"seq": target},
            device_id_type=MESH,
        ).start()

    def send_kv(plane, turn):
        target, h, slot = nearest(plane, turn)
        pltpu.make_async_remote_copy(
            src_ref=kv_out.at[h],
            dst_ref=kv_land.at[block_of(slot)],
            send_sem=kv_send,
            recv_sem=kv_recv,
            device_id={"seq": target},
            device_id_type=MESH,
        ).start()

    def send_hid(plane, turn):
        target, h, slot = nearest(plane, turn)
        pltpu.make_async_remote_copy(
            src_ref=h_in.at[:, cols_of(h)],
            dst_ref=hid_land.at[block_of(slot)],
            send_sem=hid_send,
            recv_sem=hid_recv,
            device_id={"seq": target},
            device_id_type=MESH,
        ).start()

    own_plane, all_planes = (2, 1, 3), (2, 1, 3, 0)

    pl.semaphore_wait(
        barrier,
        7 + jnp.where(z > 0, 1, 0) + jnp.where(odd, 2, 0) + jnp.where(last, 1, 0),
    )

    @pl.when(z < PLANES - 1)
    def _():
        pl.semaphore_signal(barrier, inc=1, device_id={"seq": seq + 8}, device_id_type=MESH)

    for down in (3, 2, 1):

        @pl.when(z >= down)
        def _():
            pl.semaphore_signal(
                above.at[z], inc=1, device_id={"seq": seq - 8 * down}, device_id_type=MESH
            )

    for turn in own_plane:
        send_q(z, turn)
    for apart in (1, 2, 3):
        plane = z ^ apart

        @pl.when(plane > z)
        def _():
            pl.semaphore_wait(above.at[plane], 1)

        for turn in all_planes:
            send_q(plane, turn)

    @pl.when(odd)
    def _():
        for other in (following, previous):
            pl.semaphore_signal(okay, inc=1, device_id={"section": other}, device_id_type=MESH)

    for apart in (3, 2, 1):
        for turn in all_planes:
            send_kv(z ^ apart, turn)
    for turn in own_plane:
        send_kv(z, turn)
    for apart in (3, 2, 1):
        for turn in all_planes:
            send_hid(z ^ apart, turn)
    for turn in own_plane:
        send_hid(z, turn)

    for load in loads[4:]:
        load.wait()
    patch_start = lax.rem(patch_ref[0] - section + PATCHES, PATCHES) * PATCH
    text_live = text_ref[0]
    first = side * STALE
    stale_k.wait()
    stale_v.wait()
    dead_first = jnp.logical_and(first >= patch_start, first < patch_start + PATCH)
    use_far = jnp.where(dead_first, 1.0, 0.0).astype(jnp.float32)
    spare = (
        keys[0:16, :].astype(jnp.float32)[0:1] * (1.0 - use_far)
        + keys[2048:2064, :].astype(jnp.float32)[0:1] * use_far
    )

    def mask_rows(i, carry):
        rows = pl.ds(pl.multiple_of(i * 128, 128), 128)
        position = first + i * 128 + lax.broadcasted_iota(jnp.int32, (128, DIM), 0)
        outside = jnp.logical_or(position < patch_start, position >= patch_start + PATCH)
        video = jnp.logical_and(position < VIDEO, outside)
        text = jnp.logical_and(position >= VIDEO, position - VIDEO < text_live)
        live = jnp.logical_or(video, text)
        key_rows = keys[rows, :].astype(jnp.float32)
        keys[rows, :] = jnp.where(live, key_rows, spare).astype(jnp.bfloat16)
        value_rows = vals[rows, 0:DIM].astype(jnp.float32)
        vals[rows, 0:DIM] = jnp.where(live, value_rows, 0.0).astype(jnp.bfloat16)
        vals[rows, DIM : 2 * DIM] = jnp.where(live, 1.0, 0.0).astype(jnp.bfloat16)
        return carry

    lax.fori_loop(0, STALE // 128, mask_rows, 0)
    vals[STALE:KEYS, DIM : 2 * DIM] = jnp.ones((FRESH, DIM), jnp.bfloat16)

    def attend(rows, parts, resume):
        q = q_all[rows, :]
        top = high[rows, :] if resume else None
        total = acc[rows, :] if resume else None

        def scores_of(part):
            start, count = part
            return lax.dot_general(
                q,
                keys[start : start + count, :],
                (((1,), (1,)), ((), ())),
                preferred_element_type=jnp.float32,
            )

        ahead = scores_of(parts[0])
        for n, (start, count) in enumerate(parts):
            scores = ahead
            if n + 1 < len(parts):
                ahead = scores_of(parts[n + 1])
            part_top = jnp.max(scores, axis=1, keepdims=True)
            new_top = part_top if top is None else jnp.maximum(top, part_top)
            weights = jnp.exp2((scores - new_top) * RATE).astype(jnp.bfloat16)
            summed = jnp.dot(
                weights, vals[start : start + count, :], preferred_element_type=jnp.float32
            )
            if top is not None:
                summed = total * jnp.exp2((top - new_top) * RATE) + summed
            top, total = new_top, summed
        return top, total

    def keep(rows, state):
        high[rows, :], acc[rows, :] = state

    def finished(state):
        top, total = state
        weight = total[:, DIM : 2 * DIM]
        partial = (total[:, 0:DIM] / weight).astype(jnp.bfloat16)
        return partial, top * RATE + jnp.log2(weight)

    near_base, far_base = side * SIDE_ROWS, (1 - side) * SIDE_ROWS

    def chunk_rows(base, planes):
        return pl.ds(pl.multiple_of(base + planes * ROWS, ROWS), ROWS)

    def wait_bytes(ref, sem):
        pltpu.make_async_copy(ref, ref, sem).wait()

    def pass_copy(planes):
        rows = q_all.at[chunk_rows(near_base, planes)]
        return pltpu.make_async_remote_copy(
            src_ref=rows,
            dst_ref=rows,
            send_sem=pass_send.at[planes],
            recv_sem=pass_recv.at[planes],
            device_id={"seq": partner},
            device_id_type=MESH,
        )

    def part_copy(planes):
        return pltpu.make_async_remote_copy(
            src_ref=part_out.at[planes],
            dst_ref=part_land.at[planes],
            send_sem=part_send.at[planes],
            recv_sem=part_recv.at[planes],
            device_id={"seq": partner},
            device_id_type=MESH,
        )

    def lse_copy(planes):
        return pltpu.make_async_remote_copy(
            src_ref=lse_out.at[planes],
            dst_ref=lse_land.at[planes],
            send_sem=lse_send.at[planes],
            recv_sem=lse_recv.at[planes],
            device_id={"seq": partner},
            device_id_type=MESH,
        )

    def core_copy(planes):
        return pltpu.make_async_remote_copy(
            src_ref=core_out.at[planes],
            dst_ref=core_land.at[planes],
            send_sem=core_send.at[planes],
            recv_sem=core_recv.at[planes],
            device_id={"cfg": 1 - core},
            device_id_type=MESH,
        )

    def send_fin(planes):
        for b in range(2 * NEAR):
            plane = 2 * planes + b // NEAR
            token_y = ((seq & 6) + 4 * side + b % NEAR + 5) & 7
            pltpu.make_async_remote_copy(
                src_ref=fin.at[planes, pl.ds(b * TOKENS, TOKENS)],
                dst_ref=out_ref.at[:, cols_of(head)],
                send_sem=fin_send,
                recv_sem=fin_recv,
                device_id={"section": following, "seq": (plane << 3) | token_y},
                device_id_type=MESH,
            ).start()

    def guide(planes):
        core_copy(planes).wait_recv()
        here = core_out[planes].astype(jnp.float32)
        there = core_land[planes].astype(jnp.float32)
        is_first = core == 0
        guided_side = jnp.where(is_first, here, there)
        plain_side = jnp.where(is_first, there, here)
        fin[planes] = (plain_side + GUIDE * (guided_side - plain_side)).astype(jnp.bfloat16)
        send_fin(planes)

    def combine(planes):
        lse_copy(planes).wait_recv()
        part_copy(planes).wait_recv()
        lse_here = lse_own[planes]
        lse_there = jnp.transpose(jnp.broadcast_to(lse_land[planes, 0:1, :], (DIM, ROWS)))
        joint = jnp.maximum(lse_here, lse_there)
        weight_here = jnp.exp2(lse_here - joint)
        weight_there = jnp.exp2(lse_there - joint)
        merged = part_own[planes].astype(jnp.float32) * weight_here
        merged += part_land[planes].astype(jnp.float32) * weight_there
        attended = (merged / (weight_here + weight_there)).astype(jnp.bfloat16)
        held = hid_land[pl.ds(planes * 2 * NEAR, 2 * NEAR)].reshape(ROWS, DIM)
        result = held.astype(jnp.float32) + gate * attended.astype(jnp.float32)
        result = result.astype(jnp.bfloat16)

        @pl.when(last)
        def _():
            core_out[planes] = result
            core_copy(planes).start()

        @pl.when(jnp.logical_not(last))
        def _():
            fin[planes] = result
            send_fin(planes)

    def send_part(planes, state):
        partial, lse = finished(state)
        part_out[planes] = partial
        part_copy(planes).start()
        lse_out[planes] = jnp.transpose(lse)[0:8, :]
        lse_copy(planes).start()

    def keep_part(planes, state):
        part_own[planes], lse_own[planes] = finished(state)

    def pass_on(planes):
        wait_bytes(q_all.at[chunk_rows(near_base, planes)], q_recv.at[planes])
        pass_copy(planes).start()

    one, two = z >> 1, (z >> 1) ^ 1
    near_one, near_two = chunk_rows(near_base, one), chunk_rows(near_base, two)
    far_one, far_two = chunk_rows(far_base, one), chunk_rows(far_base, two)

    pass_on(one)
    keep(near_one, attend(near_one, STALE_PARTS, False))
    pass_on(two)

    @pl.when(jnp.logical_not(odd))
    def _():
        pl.semaphore_wait(okay, 2)
        for other in (following, previous):
            pl.semaphore_signal(okay, inc=1, device_id={"section": other}, device_id_type=MESH)

    wait_bytes(q_all.at[far_one], pass_recv.at[one])
    keep(far_one, attend(far_one, STALE_PARTS, False))

    wait_bytes(kv_land, kv_recv)
    keys[STALE:KEYS, :] = kv_land[:, 0].reshape(FRESH, DIM)
    vals[STALE:KEYS, 0:DIM] = kv_land[:, 1].reshape(FRESH, DIM)
    send_part(one, attend(far_one, (FRESH_PART,), True))
    keep_part(one, attend(near_one, (FRESH_PART,), True))
    wait_bytes(q_all.at[far_two], pass_recv.at[two])
    send_part(two, attend(far_two, STALE_PARTS + (FRESH_PART,), False))

    @pl.when(odd)
    def _():
        pl.semaphore_wait(okay, 2)

    gate = gates[pl.ds(time_ref[0], 1), :]
    wait_bytes(hid_land, hid_recv)
    combine(one)
    keep(near_two, attend(near_two, STALE_PARTS[:2], False))

    @pl.when(last)
    def _():
        guide(one)

    keep_part(two, attend(near_two, STALE_PARTS[2:] + (FRESH_PART,), True))
    combine(two)

    @pl.when(last)
    def _():
        guide(two)
        for planes in range(2):
            core_copy(planes).wait_send()

    for planes in range(2):
        pass_copy(planes).wait_send()
        part_copy(planes).wait_send()
        lse_copy(planes).wait_send()
    rest = HEADS - 1
    wait_bytes(q_all.at[pl.ds(0, rest * TOKENS)], q_send)
    wait_bytes(kv_out.at[pl.ds(0, rest)], kv_send)
    wait_bytes(hid_land.at[pl.ds(0, rest)], hid_send)
    wait_bytes(fin, fin_send)
    wait_bytes(fin, fin_recv)


def body(
    hidden, queries, fresh_keys, fresh_values, stale_keys, stale_values, gate_table, timestep,
    patch_index, text_lengths,
):
    bf16, f32 = jnp.bfloat16, jnp.float32
    flat = (TOKENS, HEADS * DIM)
    dma, regular = pltpu.SemaphoreType.DMA, pltpu.SemaphoreType.REGULAR
    scratch = [
        pltpu.VMEM(flat, bf16),
        pltpu.VMEM(flat, bf16),
        pltpu.VMEM(flat, bf16),
        pltpu.VMEM(flat, bf16),
        pltpu.VMEM((HEADS, 2, TOKENS, DIM), bf16),
        pltpu.VMEM((PATCH, DIM), bf16),
        pltpu.VMEM((HEADS, 2, TOKENS, DIM), bf16),
        pltpu.VMEM((HEADS, TOKENS, DIM), bf16),
        pltpu.VMEM((KEYS, DIM), bf16),
        pltpu.VMEM((KEYS, 2 * DIM), bf16),
        pltpu.VMEM((50, DIM), f32),
        pltpu.VMEM((PATCH, 1), f32),
        pltpu.VMEM((PATCH, 2 * DIM), f32),
        pltpu.VMEM((2, ROWS, DIM), bf16),
        pltpu.VMEM((2, ROWS, DIM), bf16),
        pltpu.VMEM((2, ROWS, DIM), bf16),
        pltpu.VMEM((2, ROWS, DIM), f32),
        pltpu.VMEM((2, 8, ROWS), f32),
        pltpu.VMEM((2, 8, ROWS), f32),
        pltpu.VMEM((2, ROWS, DIM), bf16),
        pltpu.VMEM((2, ROWS, DIM), bf16),
        pltpu.VMEM((2, ROWS, DIM), bf16),
        pltpu.SMEM((1,), jnp.int32),
        pltpu.SMEM((1,), jnp.int32),
        pltpu.SMEM((1,), jnp.int32),
        dma((8,)),
        dma((2,)),
        dma,
        dma((2,)),
        dma((2,)),
        dma((2,)),
        dma,
        dma,
        dma,
        dma,
        dma((2,)),
        dma((2,)),
        dma((2,)),
        dma((2,)),
        dma((2,)),
        dma((2,)),
        dma,
        dma,
        regular((PLANES,)),
        regular,
    ]
    anywhere = pl.BlockSpec(memory_space=pl.ANY)
    out = pl.pallas_call(
        kernel,
        out_shape=pltpu.VMEM(flat, bf16),
        in_specs=[anywhere] * 10,
        out_specs=pl.BlockSpec(memory_space=pltpu.VMEM),
        scratch_shapes=scratch,
        compiler_params=pltpu.CompilerParams(
            collective_id=0, has_side_effects=True, vmem_limit_bytes=56 * 2**20
        ),
        cost_estimate=pl.CostEstimate(
            flops=4 * PATCH * KEYS * DIM, bytes_accessed=2**22, transcendentals=PATCH * KEYS
        ),
    )(
        patch_index.reshape(1),
        text_lengths,
        timestep.reshape(1),
        hidden.reshape(flat),
        queries.reshape(flat),
        fresh_keys.reshape(flat),
        fresh_values.reshape(flat),
        stale_keys.reshape(STALE, DIM),
        stale_values.reshape(STALE, DIM),
        gate_table,
    )
    return out.reshape(1, 1, TOKENS, HEADS * DIM)


def solution(mesh):
    rows = P("cfg", "section", "seq", None)
    stale = P("cfg", "section", "seq", None, None)
    return jax.shard_map(
        body,
        mesh=mesh,
        in_specs=(
            rows, rows, rows, rows, stale, stale, P(None, "section", None), P(), P(), P("cfg"),
        ),
        out_specs=rows,
        check_vma=False,
    )
```

```python
import functools
import math

import jax
import jax.numpy as jnp
from jax import lax
from jax.experimental import pallas as pl
from jax.experimental.pallas import tpu as pltpu
from jax.sharding import PartitionSpec as P

HEADS = 16
DIM = 128
PATCHES = 8
PATCH = 1024
VIDEO = 8192
GUIDE = 5.0
MESH = pl.DeviceIdType.MESH

N_SECTION = 8
TOKENS = 32
STALE = 4224
FRESH = 512
KEYS = STALE + FRESH
PLANES = 4
NEAR = 4
PLANE_ROWS = NEAR * TOKENS
ROWS = 2 * PLANE_ROWS
SIDE_ROWS = PLANES * PLANE_ROWS
STALE_PARTS = ((0, 1024), (1024, 1024), (2048, 1024), (3072, 1152))
FRESH_PART = (STALE, FRESH)
LOG2E = math.log2(math.e)
RATE = DIM**-0.5 * LOG2E


def kernel(
    patch_hbm,
    text_hbm,
    time_hbm,
    hidden_hbm,
    q_hbm,
    k_hbm,
    v_hbm,
    sk_hbm,
    sv_hbm,
    gate_hbm,
    out_ref,
    q_in,
    k_in,
    v_in,
    h_in,
    kv_out,
    q_all,
    kv_land,
    hid_land,
    keys,
    vals,
    gates,
    high,
    acc,
    part_out,
    part_own,
    part_land,
    lse_own,
    lse_out,
    lse_land,
    fin,
    core_land,
    patch_ref,
    text_ref,
    time_ref,
    in_sem,
    stale_sem,
    q_send,
    q_recv,
    pass_send,
    pass_recv,
    kv_send,
    kv_recv,
    hid_send,
    hid_recv,
    part_send,
    part_recv,
    lse_send,
    lse_recv,
    core_send,
    core_recv,
    fin_send,
    fin_recv,
    above,
    okay,
):
    section = lax.axis_index("section")
    seq = lax.axis_index("seq")
    core = lax.axis_index("cfg")
    z = seq >> 3
    y = seq & 7
    head = seq >> 1
    side = seq & 1
    partner = seq ^ 1
    following = (section + 1) & 7
    previous = (section + 7) & 7
    odd = (section & 1) == 1
    first_section = section == 0

    def cols_of(h):
        return pl.ds(pl.multiple_of(h * DIM, DIM), DIM)

    barrier = pltpu.get_barrier_semaphore()
    for step in (4, 3, 5, 2, 6, 1, 7):
        pl.semaphore_signal(
            barrier, inc=1, device_id={"seq": (z << 3) | ((y + step) & 7)}, device_id_type=MESH
        )

    @pl.when(jnp.logical_not(odd))
    def _():
        for other in (following, previous):
            pl.semaphore_signal(
                barrier, inc=1, device_id={"section": other}, device_id_type=MESH
            )

    @pl.when(first_section)
    def _():
        pl.semaphore_signal(barrier, inc=1, device_id={"cfg": 1 - core}, device_id_type=MESH)

    loads = [
        pltpu.make_async_copy(src, dst, in_sem.at[i])
        for i, (src, dst) in enumerate(
            [
                (q_hbm, q_in),
                (k_hbm, k_in),
                (v_hbm, v_in),
                (hidden_hbm, h_in),
                (gate_hbm.at[:, 0, cols_of(head)], gates),
                (patch_hbm, patch_ref),
                (text_hbm, text_ref),
                (time_hbm, time_ref),
            ]
        )
    ]
    for load in loads:
        load.start()
    stale_k = pltpu.make_async_copy(sk_hbm, keys.at[pl.ds(0, STALE)], stale_sem.at[0])
    stale_v = pltpu.make_async_copy(
        sv_hbm, vals.at[pl.ds(0, STALE), pl.ds(0, DIM)], stale_sem.at[1]
    )
    stale_k.start()
    stale_v.start()

    def slot_of(pair):
        return (y - pair + 3) & 7

    def nearest(plane, turn):
        pair = (plane << 3) | ((y + 2 * turn) & 6)
        slot = slot_of(pair)
        return pair | (slot >> 2), pair >> 1, slot

    def q_rows(slot):
        start = (slot >> 2) * SIDE_ROWS + z * PLANE_ROWS + (slot & 3) * TOKENS
        return pl.ds(pl.multiple_of(start, TOKENS), TOKENS)

    def block_of(slot):
        return z * NEAR + (slot & 3)

    mine = slot_of(seq & 30)
    own_q = pltpu.make_async_copy(
        q_in.at[:, cols_of(head)], q_all.at[q_rows(mine)], q_recv.at[z >> 1]
    )
    own_kv = pltpu.make_async_copy(kv_out.at[head], kv_land.at[block_of(mine)], kv_recv)
    own_hid = pltpu.make_async_copy(
        h_in.at[:, cols_of(head)], hid_land.at[block_of(mine)], hid_recv.at[z >> 1]
    )

    def send_q(plane, turn):
        target, h, slot = nearest(plane, turn)
        pltpu.make_async_remote_copy(
            src_ref=q_in.at[:, cols_of(h)],
            dst_ref=q_all.at[q_rows(slot)],
            send_sem=q_send,
            recv_sem=q_recv.at[z >> 1],
            device_id={"seq": target},
            device_id_type=MESH,
        ).start()

    def send_kv(plane, turn):
        target, h, slot = nearest(plane, turn)
        pltpu.make_async_remote_copy(
            src_ref=kv_out.at[h],
            dst_ref=kv_land.at[block_of(slot)],
            send_sem=kv_send,
            recv_sem=kv_recv,
            device_id={"seq": target},
            device_id_type=MESH,
        ).start()

    def send_hid(plane, turn):
        target, h, slot = nearest(plane, turn)
        pltpu.make_async_remote_copy(
            src_ref=h_in.at[:, cols_of(h)],
            dst_ref=hid_land.at[block_of(slot)],
            send_sem=hid_send,
            recv_sem=hid_recv.at[z >> 1],
            device_id={"seq": target},
            device_id_type=MESH,
        ).start()

    own_plane, all_planes = (2, 1, 3), (2, 1, 3, 0)

    pl.semaphore_wait(
        barrier,
        7 + jnp.where(z > 0, 1, 0) + jnp.where(odd, 2, 0) + jnp.where(first_section, 1, 0),
    )

    @pl.when(z < PLANES - 1)
    def _():
        pl.semaphore_signal(barrier, inc=1, device_id={"seq": seq + 8}, device_id_type=MESH)

    for down in (3, 2, 1):

        @pl.when(z >= down)
        def _():
            pl.semaphore_signal(
                above.at[z], inc=1, device_id={"seq": seq - 8 * down}, device_id_type=MESH
            )

    def hear(plane):
        @pl.when(plane > z)
        def _():
            pl.semaphore_wait(above.at[plane], 1)

    def send_to(send, plane):
        for turn in all_planes:
            send(plane, turn)

    def lay_out():
        loads[1].wait()
        loads[2].wait()
        for h in range(HEADS):
            kv_out[h, 0] = k_in[:, h * DIM : (h + 1) * DIM]
            kv_out[h, 1] = v_in[:, h * DIM : (h + 1) * DIM]
        own_kv.start()

    def start_q():
        loads[0].wait()
        own_q.start()

    def send_own(send):
        for turn in own_plane:
            send(z, turn)

    def greet_back():
        @pl.when(odd)
        def _():
            for other in (following, previous):
                pl.semaphore_signal(
                    okay, inc=1, device_id={"section": other}, device_id_type=MESH
                )

    def send_all_hid():
        loads[3].wait()
        own_hid.start()
        for turn in all_planes:
            for apart in (3, 0, 2, 1):
                if apart or turn:
                    send_hid(z ^ apart, turn)

    start_q()
    send_own(send_q)
    for n in range(PLANES - 1):
        plane = n + jnp.where(z <= n, 1, 0)
        hear(plane)
        send_to(send_q, plane)
    greet_back()
    lay_out()
    for turn in all_planes:
        for apart in (3, 0, 2, 1):
            if apart or turn:
                send_kv(z ^ apart, turn)
    for load in loads[4:]:
        load.wait()
    patch_start = lax.rem(patch_ref[0] - section + PATCHES, PATCHES) * PATCH
    text_live = text_ref[0]
    first = side * STALE
    stale_k.wait()
    stale_v.wait()
    dead_first = jnp.logical_and(first >= patch_start, first < patch_start + PATCH)
    use_far = jnp.where(dead_first, 1.0, 0.0).astype(jnp.float32)
    spare = (
        keys[0:16, :].astype(jnp.float32)[0:1] * (1.0 - use_far)
        + keys[2048:2064, :].astype(jnp.float32)[0:1] * use_far
    )

    def mask_rows(i, carry):
        rows = pl.ds(pl.multiple_of(i * 128, 128), 128)
        position = first + i * 128 + lax.broadcasted_iota(jnp.int32, (128, DIM), 0)
        outside = jnp.logical_or(position < patch_start, position >= patch_start + PATCH)
        video = jnp.logical_and(position < VIDEO, outside)
        text = jnp.logical_and(position >= VIDEO, position - VIDEO < text_live)
        live = jnp.logical_or(video, text)
        key_rows = keys[rows, :].astype(jnp.float32)
        keys[rows, :] = jnp.where(live, key_rows, spare).astype(jnp.bfloat16)
        value_rows = vals[rows, 0:DIM].astype(jnp.float32)
        vals[rows, 0:DIM] = jnp.where(live, value_rows, 0.0).astype(jnp.bfloat16)
        vals[rows, DIM : 2 * DIM] = jnp.where(live, 1.0, 0.0).astype(jnp.bfloat16)
        return carry

    lax.fori_loop(0, STALE // 128, mask_rows, 0)
    vals[STALE:KEYS, DIM : 2 * DIM] = jnp.ones((FRESH, DIM), jnp.bfloat16)

    def attend(rows, parts, resume):
        q = q_all[rows, :]
        top = high[rows, :] if resume else None
        total = acc[rows, :] if resume else None

        def scores_of(part):
            start, count = part
            return lax.dot_general(
                q,
                keys[start : start + count, :],
                (((1,), (1,)), ((), ())),
                preferred_element_type=jnp.float32,
            )

        ahead = scores_of(parts[0])
        for n, (start, count) in enumerate(parts):
            scores = ahead
            if n + 1 < len(parts):
                ahead = scores_of(parts[n + 1])
            part_top = jnp.max(scores, axis=1, keepdims=True)
            new_top = part_top if top is None else jnp.maximum(top, part_top)
            weights = jnp.exp2((scores - new_top) * RATE).astype(jnp.bfloat16)
            summed = jnp.dot(
                weights, vals[start : start + count, :], preferred_element_type=jnp.float32
            )
            if top is not None:
                summed = total * jnp.exp2((top - new_top) * RATE) + summed
            top, total = new_top, summed
        return top, total

    def keep(rows, state):
        high[rows, :], acc[rows, :] = state

    def finished(state):
        top, total = state
        weight = total[:, DIM : 2 * DIM]
        partial = (total[:, 0:DIM] / weight).astype(jnp.bfloat16)
        return partial, top * RATE + jnp.log2(weight)

    near_base, far_base = side * SIDE_ROWS, (1 - side) * SIDE_ROWS

    def chunk_rows(base, planes):
        return pl.ds(pl.multiple_of(base + planes * ROWS, ROWS), ROWS)

    def wait_bytes(ref, sem):
        pltpu.make_async_copy(ref, ref, sem).wait()

    def pass_copy(planes):
        rows = q_all.at[chunk_rows(near_base, planes)]
        return pltpu.make_async_remote_copy(
            src_ref=rows,
            dst_ref=rows,
            send_sem=pass_send.at[planes],
            recv_sem=pass_recv.at[planes],
            device_id={"seq": partner},
            device_id_type=MESH,
        )

    def part_copy(planes):
        return pltpu.make_async_remote_copy(
            src_ref=part_out.at[planes],
            dst_ref=part_land.at[planes],
            send_sem=part_send.at[planes],
            recv_sem=part_recv.at[planes],
            device_id={"seq": partner},
            device_id_type=MESH,
        )

    def lse_copy(planes):
        return pltpu.make_async_remote_copy(
            src_ref=lse_out.at[planes],
            dst_ref=lse_land.at[planes],
            send_sem=lse_send.at[planes],
            recv_sem=lse_recv.at[planes],
            device_id={"seq": partner},
            device_id_type=MESH,
        )

    def send_fin(planes):
        first_y = ((seq & 6) + 4 * side + 5) & 7
        turned = jnp.where(first_y == 5, 3, 0)
        for b in range(2 * NEAR):
            plane = 2 * planes + b // NEAR
            place = (b % NEAR) ^ turned
            token_y = (first_y + place) & 7
            start = (b // NEAR) * NEAR * TOKENS + place * TOKENS
            pltpu.make_async_remote_copy(
                src_ref=fin.at[planes, pl.ds(pl.multiple_of(start, TOKENS), TOKENS)],
                dst_ref=out_ref.at[:, cols_of(head)],
                send_sem=fin_send,
                recv_sem=fin_recv,
                device_id={"section": following, "seq": (plane << 3) | token_y},
                device_id_type=MESH,
            ).start()

    def combine(planes):
        lse_copy(planes).wait_recv()
        part_copy(planes).wait_recv()
        lse_here = lse_own[planes]
        lse_there = jnp.transpose(jnp.broadcast_to(lse_land[planes, 0:1, :], (DIM, ROWS)))
        joint = jnp.maximum(lse_here, lse_there)
        weight_here = jnp.exp2(lse_here - joint)
        weight_there = jnp.exp2(lse_there - joint)
        merged = part_own[planes].astype(jnp.float32) * weight_here
        merged += part_land[planes].astype(jnp.float32) * weight_there
        attended = (merged / (weight_here + weight_there)).astype(jnp.bfloat16)
        blocks = pl.ds(planes * 2 * NEAR, 2 * NEAR)
        wait_bytes(hid_land.at[blocks], hid_recv.at[planes])
        held = hid_land[blocks].reshape(ROWS, DIM)
        result = held.astype(jnp.float32) + gate * attended.astype(jnp.float32)
        result = result.astype(jnp.bfloat16)

        fin[planes] = result
        send_fin(planes)

    def send_part(planes, state):
        partial, lse = finished(state)
        part_out[planes] = partial
        part_copy(planes).start()
        lse_out[planes] = jnp.transpose(lse)[0:8, :]
        lse_copy(planes).start()

    def keep_part(planes, state):
        part_own[planes], lse_own[planes] = finished(state)

    def pass_on(planes):
        wait_bytes(q_all.at[chunk_rows(near_base, planes)], q_recv.at[planes])
        pass_copy(planes).start()

    one, two = 0, 1
    near_one, near_two = chunk_rows(near_base, one), chunk_rows(near_base, two)
    far_one, far_two = chunk_rows(far_base, one), chunk_rows(far_base, two)

    pass_on(one)
    keep(near_one, attend(near_one, STALE_PARTS, False))
    pass_on(two)

    @pl.when(jnp.logical_not(odd))
    def _():
        pl.semaphore_wait(okay, 2)
        for other in (following, previous):
            pl.semaphore_signal(okay, inc=1, device_id={"section": other}, device_id_type=MESH)

    wait_bytes(q_all.at[far_one], pass_recv.at[one])
    keep(far_one, attend(far_one, STALE_PARTS, False))

    wait_bytes(kv_land, kv_recv)
    keys[STALE:KEYS, :] = kv_land[:, 0].reshape(FRESH, DIM)
    vals[STALE:KEYS, 0:DIM] = kv_land[:, 1].reshape(FRESH, DIM)
    send_part(one, attend(far_one, (FRESH_PART,), True))

    send_all_hid()
    keep_part(one, attend(near_one, (FRESH_PART,), True))
    wait_bytes(q_all.at[far_two], pass_recv.at[two])
    send_part(two, attend(far_two, STALE_PARTS + (FRESH_PART,), False))

    @pl.when(odd)
    def _():
        pl.semaphore_wait(okay, 2)

    gate = gates[pl.ds(time_ref[0], 1), :]
    combine(one)

    keep_part(two, attend(near_two, STALE_PARTS + (FRESH_PART,), False))
    combine(two)

    for planes in range(2):
        pass_copy(planes).wait_send()
        part_copy(planes).wait_send()
        lse_copy(planes).wait_send()
    rest = HEADS - 1
    wait_bytes(q_all.at[pl.ds(0, rest * TOKENS)], q_send)
    wait_bytes(kv_out.at[pl.ds(0, rest)], kv_send)
    wait_bytes(hid_land.at[pl.ds(0, rest)], hid_send)
    wait_bytes(fin, fin_send)
    wait_bytes(fin, fin_recv)

    @pl.when(first_section)
    def _():
        swap = pltpu.make_async_remote_copy(
            src_ref=out_ref,
            dst_ref=core_land,
            send_sem=core_send,
            recv_sem=core_recv,
            device_id={"cfg": 1 - core},
            device_id_type=MESH,
        )
        swap.start()
        swap.wait()
        here = out_ref[...].astype(jnp.float32)
        there = core_land[...].astype(jnp.float32)
        is_first = core == 0
        guided_side = jnp.where(is_first, here, there)
        plain_side = jnp.where(is_first, there, here)
        out_ref[...] = (plain_side + GUIDE * (guided_side - plain_side)).astype(jnp.bfloat16)


def body(
    hidden, queries, fresh_keys, fresh_values, stale_keys, stale_values, gate_table, timestep,
    patch_index, text_lengths,
):
    bf16, f32 = jnp.bfloat16, jnp.float32
    flat = (TOKENS, HEADS * DIM)
    dma, regular = pltpu.SemaphoreType.DMA, pltpu.SemaphoreType.REGULAR
    scratch = [
        pltpu.VMEM(flat, bf16),
        pltpu.VMEM(flat, bf16),
        pltpu.VMEM(flat, bf16),
        pltpu.VMEM(flat, bf16),
        pltpu.VMEM((HEADS, 2, TOKENS, DIM), bf16),
        pltpu.VMEM((PATCH, DIM), bf16),
        pltpu.VMEM((HEADS, 2, TOKENS, DIM), bf16),
        pltpu.VMEM((HEADS, TOKENS, DIM), bf16),
        pltpu.VMEM((KEYS, DIM), bf16),
        pltpu.VMEM((KEYS, 2 * DIM), bf16),
        pltpu.VMEM((50, DIM), f32),
        pltpu.VMEM((PATCH, 1), f32),
        pltpu.VMEM((PATCH, 2 * DIM), f32),
        pltpu.VMEM((2, ROWS, DIM), bf16),
        pltpu.VMEM((2, ROWS, DIM), bf16),
        pltpu.VMEM((2, ROWS, DIM), bf16),
        pltpu.VMEM((2, ROWS, DIM), f32),
        pltpu.VMEM((2, 8, ROWS), f32),
        pltpu.VMEM((2, 8, ROWS), f32),
        pltpu.VMEM((2, ROWS, DIM), bf16),
        pltpu.VMEM(flat, bf16),
        pltpu.SMEM((1,), jnp.int32),
        pltpu.SMEM((1,), jnp.int32),
        pltpu.SMEM((1,), jnp.int32),
        dma((8,)),
        dma((2,)),
        dma,
        dma((2,)),
        dma((2,)),
        dma((2,)),
        dma,
        dma,
        dma,
        dma((2,)),
        dma((2,)),
        dma((2,)),
        dma((2,)),
        dma((2,)),
        dma,
        dma,
        dma,
        dma,
        regular((PLANES,)),
        regular,
    ]
    anywhere = pl.BlockSpec(memory_space=pl.ANY)
    out = pl.pallas_call(
        kernel,
        out_shape=pltpu.VMEM(flat, bf16),
        in_specs=[anywhere] * 10,
        out_specs=pl.BlockSpec(memory_space=pltpu.VMEM),
        scratch_shapes=scratch,
        compiler_params=pltpu.CompilerParams(
            collective_id=0, has_side_effects=True, vmem_limit_bytes=56 * 2**20
        ),
        cost_estimate=pl.CostEstimate(
            flops=4 * PATCH * KEYS * DIM, bytes_accessed=2**22, transcendentals=PATCH * KEYS
        ),
    )(
        patch_index.reshape(1),
        text_lengths,
        timestep.reshape(1),
        hidden.reshape(flat),
        queries.reshape(flat),
        fresh_keys.reshape(flat),
        fresh_values.reshape(flat),
        stale_keys.reshape(STALE, DIM),
        stale_values.reshape(STALE, DIM),
        gate_table,
    )
    return out.reshape(1, 1, TOKENS, HEADS * DIM)


def solution(mesh):
    rows = P("cfg", "section", "seq", None)
    stale = P("cfg", "section", "seq", None, None)
    return jax.shard_map(
        body,
        mesh=mesh,
        in_specs=(
            rows, rows, rows, rows, stale, stale, P(None, "section", None), P(), P(), P("cfg"),
        ),
        out_specs=rows,
        check_vma=False,
    )
```

```python
import functools
import math

import jax
import jax.numpy as jnp
from jax import lax
from jax.experimental import pallas as pl
from jax.experimental.pallas import tpu as pltpu
from jax.sharding import PartitionSpec as P

HEADS = 16
DIM = 128
PATCHES = 8
PATCH = 1024
VIDEO = 8192
GUIDE = 5.0
MESH = pl.DeviceIdType.MESH

N_SECTION = 8
TOKENS = 32
STALE = 4224
FRESH = 512
KEYS = STALE + FRESH
PLANES = 4
NEAR = 4
PLANE_ROWS = NEAR * TOKENS
ROWS = 2 * PLANE_ROWS
SIDE_ROWS = PLANES * PLANE_ROWS
STALE_PARTS = ((0, 1024), (1024, 1024), (2048, 1024), (3072, 1152))
FRESH_PART = (STALE, FRESH)
LOG2E = math.log2(math.e)
RATE = DIM**-0.5 * LOG2E


def kernel(
    patch_hbm,
    text_hbm,
    time_hbm,
    hidden_hbm,
    q_hbm,
    k_hbm,
    v_hbm,
    sk_hbm,
    sv_hbm,
    gate_hbm,
    out_ref,
    q_in,
    k_in,
    v_in,
    h_in,
    kv_out,
    q_all,
    kv_land,
    hid_land,
    keys,
    vals,
    gates,
    high,
    acc,
    part_out,
    part_own,
    part_land,
    lse_own,
    lse_out,
    lse_land,
    fin,
    core_land,
    patch_ref,
    text_ref,
    time_ref,
    in_sem,
    stale_sem,
    q_send,
    q_recv,
    pass_send,
    pass_recv,
    kv_send,
    kv_recv,
    hid_send,
    hid_recv,
    part_send,
    part_recv,
    lse_send,
    lse_recv,
    core_send,
    core_recv,
    fin_send,
    fin_recv,
    above,
    okay,
):
    section = lax.axis_index("section")
    seq = lax.axis_index("seq")
    core = lax.axis_index("cfg")
    z = seq >> 3
    y = seq & 7
    head = seq >> 1
    side = seq & 1
    partner = seq ^ 1
    following = (section + 1) & 7
    previous = (section + 7) & 7
    odd = (section & 1) == 1
    first_section = section == 0

    def cols_of(h):
        return pl.ds(pl.multiple_of(h * DIM, DIM), DIM)

    barrier = pltpu.get_barrier_semaphore()
    for step in (4, 3, 5, 2, 6, 1, 7):
        pl.semaphore_signal(
            barrier, inc=1, device_id={"seq": (z << 3) | ((y + step) & 7)}, device_id_type=MESH
        )

    @pl.when(jnp.logical_not(odd))
    def _():
        for other in (following, previous):
            pl.semaphore_signal(
                barrier, inc=1, device_id={"section": other}, device_id_type=MESH
            )

    @pl.when(first_section)
    def _():
        pl.semaphore_signal(barrier, inc=1, device_id={"cfg": 1 - core}, device_id_type=MESH)

    loads = [
        pltpu.make_async_copy(src, dst, in_sem.at[i])
        for i, (src, dst) in enumerate(
            [
                (q_hbm, q_in),
                (k_hbm, k_in),
                (v_hbm, v_in),
                (hidden_hbm, h_in),
                (gate_hbm.at[:, 0, cols_of(head)], gates),
                (patch_hbm, patch_ref),
                (text_hbm, text_ref),
                (time_hbm, time_ref),
            ]
        )
    ]
    for load in loads:
        load.start()
    stale_k = pltpu.make_async_copy(sk_hbm, keys.at[pl.ds(0, STALE)], stale_sem.at[0])
    stale_v = pltpu.make_async_copy(
        sv_hbm, vals.at[pl.ds(0, STALE), pl.ds(0, DIM)], stale_sem.at[1]
    )
    stale_k.start()
    stale_v.start()

    def slot_of(pair):
        return (y - pair + 3) & 7

    def nearest(plane, turn):
        pair = (plane << 3) | ((y + 2 * turn) & 6)
        slot = slot_of(pair)
        return pair | (slot >> 2), pair >> 1, slot

    def q_rows(slot):
        start = (slot >> 2) * SIDE_ROWS + z * PLANE_ROWS + (slot & 3) * TOKENS
        return pl.ds(pl.multiple_of(start, TOKENS), TOKENS)

    def block_of(slot):
        return z * NEAR + (slot & 3)

    mine = slot_of(seq & 30)
    own_q = pltpu.make_async_copy(
        q_in.at[:, cols_of(head)], q_all.at[q_rows(mine)], q_recv.at[z >> 1]
    )
    own_kv = pltpu.make_async_copy(kv_out.at[head], kv_land.at[block_of(mine)], kv_recv)
    own_hid = pltpu.make_async_copy(
        h_in.at[:, cols_of(head)], hid_land.at[block_of(mine)], hid_recv.at[z >> 1]
    )

    def send_q(plane, turn):
        target, h, slot = nearest(plane, turn)
        pltpu.make_async_remote_copy(
            src_ref=q_in.at[:, cols_of(h)],
            dst_ref=q_all.at[q_rows(slot)],
            send_sem=q_send,
            recv_sem=q_recv.at[z >> 1],
            device_id={"seq": target},
            device_id_type=MESH,
        ).start()

    def send_kv(plane, turn):
        target, h, slot = nearest(plane, turn)
        pltpu.make_async_remote_copy(
            src_ref=kv_out.at[h],
            dst_ref=kv_land.at[block_of(slot)],
            send_sem=kv_send,
            recv_sem=kv_recv,
            device_id={"seq": target},
            device_id_type=MESH,
        ).start()

    def send_hid(plane, turn):
        target, h, slot = nearest(plane, turn)
        pltpu.make_async_remote_copy(
            src_ref=h_in.at[:, cols_of(h)],
            dst_ref=hid_land.at[block_of(slot)],
            send_sem=hid_send,
            recv_sem=hid_recv.at[z >> 1],
            device_id={"seq": target},
            device_id_type=MESH,
        ).start()

    own_plane, all_planes = (2, 1, 3), (2, 1, 3, 0)

    pl.semaphore_wait(
        barrier,
        7 + jnp.where(z > 0, 1, 0) + jnp.where(odd, 2, 0) + jnp.where(first_section, 1, 0),
    )

    @pl.when(z < PLANES - 1)
    def _():
        pl.semaphore_signal(barrier, inc=1, device_id={"seq": seq + 8}, device_id_type=MESH)

    for down in (3, 2, 1):

        @pl.when(z >= down)
        def _():
            pl.semaphore_signal(
                above.at[z], inc=1, device_id={"seq": seq - 8 * down}, device_id_type=MESH
            )

    def hear(plane):
        @pl.when(plane > z)
        def _():
            pl.semaphore_wait(above.at[plane], 1)

    def send_to(send, plane):
        for turn in all_planes:
            send(plane, turn)

    def lay_out():
        loads[1].wait()
        loads[2].wait()
        for h in range(HEADS):
            kv_out[h, 0] = k_in[:, h * DIM : (h + 1) * DIM]
            kv_out[h, 1] = v_in[:, h * DIM : (h + 1) * DIM]
        own_kv.start()

    def start_q():
        loads[0].wait()
        own_q.start()

    def send_own(send):
        for turn in own_plane:
            send(z, turn)

    def greet_back():
        @pl.when(odd)
        def _():
            for other in (following, previous):
                pl.semaphore_signal(
                    okay, inc=1, device_id={"section": other}, device_id_type=MESH
                )

    def send_all_hid():
        loads[3].wait()
        own_hid.start()
        for turn in all_planes:
            for apart in (3, 0, 2, 1):
                if apart or turn:
                    send_hid(z ^ apart, turn)

    start_q()
    send_own(send_q)
    for n in range(PLANES - 1):
        plane = n + jnp.where(z <= n, 1, 0)
        hear(plane)
        send_to(send_q, plane)
    greet_back()
    lay_out()
    for turn in all_planes:
        for apart in (3, 0, 2, 1):
            if apart or turn:
                send_kv(z ^ apart, turn)
    for load in loads[4:]:
        load.wait()
    patch_start = lax.rem(patch_ref[0] - section + PATCHES, PATCHES) * PATCH
    text_live = text_ref[0]
    first = side * STALE
    stale_k.wait()
    stale_v.wait()
    dead_first = jnp.logical_and(first >= patch_start, first < patch_start + PATCH)
    use_far = jnp.where(dead_first, 1.0, 0.0).astype(jnp.float32)
    spare = (
        keys[0:16, :].astype(jnp.float32)[0:1] * (1.0 - use_far)
        + keys[2048:2064, :].astype(jnp.float32)[0:1] * use_far
    )

    def mask_rows(i, carry):
        rows = pl.ds(pl.multiple_of(i * 128, 128), 128)
        position = first + i * 128 + lax.broadcasted_iota(jnp.int32, (128, DIM), 0)
        outside = jnp.logical_or(position < patch_start, position >= patch_start + PATCH)
        video = jnp.logical_and(position < VIDEO, outside)
        text = jnp.logical_and(position >= VIDEO, position - VIDEO < text_live)
        live = jnp.logical_or(video, text)
        key_rows = keys[rows, :].astype(jnp.float32)
        keys[rows, :] = jnp.where(live, key_rows, spare).astype(jnp.bfloat16)
        value_rows = vals[rows, 0:DIM].astype(jnp.float32)
        vals[rows, 0:DIM] = jnp.where(live, value_rows, 0.0).astype(jnp.bfloat16)
        vals[rows, DIM : 2 * DIM] = jnp.where(live, 1.0, 0.0).astype(jnp.bfloat16)
        return carry

    lax.fori_loop(0, STALE // 128, mask_rows, 0)
    vals[STALE:KEYS, DIM : 2 * DIM] = jnp.ones((FRESH, DIM), jnp.bfloat16)

    def attend(rows, parts, resume):
        q = q_all[rows, :]
        top = high[rows, :] if resume else None
        total = acc[rows, :] if resume else None

        def scores_of(part):
            start, count = part
            return lax.dot_general(
                q,
                keys[start : start + count, :],
                (((1,), (1,)), ((), ())),
                preferred_element_type=jnp.float32,
            )

        ahead = scores_of(parts[0])
        for n, (start, count) in enumerate(parts):
            scores = ahead
            if n + 1 < len(parts):
                ahead = scores_of(parts[n + 1])
            part_top = jnp.max(scores, axis=1, keepdims=True)
            new_top = part_top if top is None else jnp.maximum(top, part_top)
            weights = jnp.exp2((scores - new_top) * RATE).astype(jnp.bfloat16)
            summed = jnp.dot(
                weights, vals[start : start + count, :], preferred_element_type=jnp.float32
            )
            if top is not None:
                summed = total * jnp.exp2((top - new_top) * RATE) + summed
            top, total = new_top, summed
        return top, total

    def keep(rows, state):
        high[rows, :], acc[rows, :] = state

    def finished(state):
        top, total = state
        weight = total[:, DIM : 2 * DIM]
        partial = (total[:, 0:DIM] / weight).astype(jnp.bfloat16)
        return partial, top * RATE + jnp.log2(weight)

    near_base, far_base = side * SIDE_ROWS, (1 - side) * SIDE_ROWS

    def chunk_rows(base, planes):
        return pl.ds(pl.multiple_of(base + planes * ROWS, ROWS), ROWS)

    def wait_bytes(ref, sem):
        pltpu.make_async_copy(ref, ref, sem).wait()

    def pass_copy(planes):
        rows = q_all.at[chunk_rows(near_base, planes)]
        return pltpu.make_async_remote_copy(
            src_ref=rows,
            dst_ref=rows,
            send_sem=pass_send.at[planes],
            recv_sem=pass_recv.at[planes],
            device_id={"seq": partner},
            device_id_type=MESH,
        )

    def part_copy(planes):
        return pltpu.make_async_remote_copy(
            src_ref=part_out.at[planes],
            dst_ref=part_land.at[planes],
            send_sem=part_send.at[planes],
            recv_sem=part_recv.at[planes],
            device_id={"seq": partner},
            device_id_type=MESH,
        )

    def lse_copy(planes):
        return pltpu.make_async_remote_copy(
            src_ref=lse_out.at[planes],
            dst_ref=lse_land.at[planes],
            send_sem=lse_send.at[planes],
            recv_sem=lse_recv.at[planes],
            device_id={"seq": partner},
            device_id_type=MESH,
        )

    def send_fin(planes):
        first_y = ((seq & 6) + 4 * side + 5) & 7
        turned = jnp.where(first_y == 5, 3, 0)
        for b in range(2 * NEAR):
            plane = 2 * planes + b // NEAR
            place = (b % NEAR) ^ turned
            token_y = (first_y + place) & 7
            start = (b // NEAR) * NEAR * TOKENS + place * TOKENS
            pltpu.make_async_remote_copy(
                src_ref=fin.at[planes, pl.ds(pl.multiple_of(start, TOKENS), TOKENS)],
                dst_ref=out_ref.at[:, cols_of(head)],
                send_sem=fin_send,
                recv_sem=fin_recv.at[z],
                device_id={"section": following, "seq": (plane << 3) | token_y},
                device_id_type=MESH,
            ).start()

    def combine(planes):
        lse_copy(planes).wait_recv()
        part_copy(planes).wait_recv()
        lse_here = lse_own[planes]
        lse_there = jnp.transpose(jnp.broadcast_to(lse_land[planes, 0:1, :], (DIM, ROWS)))
        joint = jnp.maximum(lse_here, lse_there)
        weight_here = jnp.exp2(lse_here - joint)
        weight_there = jnp.exp2(lse_there - joint)
        merged = part_own[planes].astype(jnp.float32) * weight_here
        merged += part_land[planes].astype(jnp.float32) * weight_there
        attended = (merged / (weight_here + weight_there)).astype(jnp.bfloat16)
        blocks = pl.ds(planes * 2 * NEAR, 2 * NEAR)
        wait_bytes(hid_land.at[blocks], hid_recv.at[planes])
        held = hid_land[blocks].reshape(ROWS, DIM)
        result = held.astype(jnp.float32) + gate * attended.astype(jnp.float32)
        result = result.astype(jnp.bfloat16)

        fin[planes] = result
        send_fin(planes)

    def send_part(planes, state):
        partial, lse = finished(state)
        part_out[planes] = partial
        part_copy(planes).start()
        lse_out[planes] = jnp.transpose(lse)[0:8, :]
        lse_copy(planes).start()

    def keep_part(planes, state):
        part_own[planes], lse_own[planes] = finished(state)

    def pass_on(planes):
        wait_bytes(q_all.at[chunk_rows(near_base, planes)], q_recv.at[planes])
        pass_copy(planes).start()

    one, two = 0, 1
    near_one, near_two = chunk_rows(near_base, one), chunk_rows(near_base, two)
    far_one, far_two = chunk_rows(far_base, one), chunk_rows(far_base, two)

    pass_on(one)
    keep(near_one, attend(near_one, STALE_PARTS, False))
    pass_on(two)

    @pl.when(jnp.logical_not(odd))
    def _():
        pl.semaphore_wait(okay, 2)
        for other in (following, previous):
            pl.semaphore_signal(okay, inc=1, device_id={"section": other}, device_id_type=MESH)

    wait_bytes(q_all.at[far_one], pass_recv.at[one])
    keep(far_one, attend(far_one, STALE_PARTS, False))

    wait_bytes(kv_land, kv_recv)
    keys[STALE:KEYS, :] = kv_land[:, 0].reshape(FRESH, DIM)
    vals[STALE:KEYS, 0:DIM] = kv_land[:, 1].reshape(FRESH, DIM)
    send_part(one, attend(far_one, (FRESH_PART,), True))

    send_all_hid()
    keep_part(one, attend(near_one, (FRESH_PART,), True))
    wait_bytes(q_all.at[far_two], pass_recv.at[two])
    send_part(two, attend(far_two, STALE_PARTS + (FRESH_PART,), False))

    @pl.when(odd)
    def _():
        pl.semaphore_wait(okay, 2)

    gate = gates[pl.ds(time_ref[0], 1), :]
    combine(one)

    keep_part(two, attend(near_two, STALE_PARTS + (FRESH_PART,), False))
    combine(two)

    for planes in range(2):
        pass_copy(planes).wait_send()
        part_copy(planes).wait_send()
        lse_copy(planes).wait_send()
    rest = HEADS - 1
    wait_bytes(q_all.at[pl.ds(0, rest * TOKENS)], q_send)
    wait_bytes(kv_out.at[pl.ds(0, rest)], kv_send)
    wait_bytes(hid_land.at[pl.ds(0, rest)], hid_send)
    def heads_of(plane):
        return (slice(None), pl.ds(plane * NEAR * DIM, NEAR * DIM))

    def swap(plane):
        return pltpu.make_async_remote_copy(
            src_ref=out_ref.at[heads_of(plane)],
            dst_ref=core_land.at[heads_of(plane)],
            send_sem=core_send.at[plane],
            recv_sem=core_recv.at[plane],
            device_id={"cfg": 1 - core},
            device_id_type=MESH,
        )

    for plane in range(PLANES):
        wait_bytes(out_ref.at[heads_of(plane)], fin_recv.at[plane])

        @pl.when(first_section)
        def _():
            swap(plane).start()

    @pl.when(first_section)
    def _():
        for plane in range(PLANES):
            swap(plane).wait()
            here = out_ref[heads_of(plane)].astype(jnp.float32)
            there = core_land[heads_of(plane)].astype(jnp.float32)
            is_first = core == 0
            guided_side = jnp.where(is_first, here, there)
            plain_side = jnp.where(is_first, there, here)
            guided = plain_side + GUIDE * (guided_side - plain_side)
            out_ref[heads_of(plane)] = guided.astype(jnp.bfloat16)

    wait_bytes(fin, fin_send)


def body(
    hidden, queries, fresh_keys, fresh_values, stale_keys, stale_values, gate_table, timestep,
    patch_index, text_lengths,
):
    bf16, f32 = jnp.bfloat16, jnp.float32
    flat = (TOKENS, HEADS * DIM)
    dma, regular = pltpu.SemaphoreType.DMA, pltpu.SemaphoreType.REGULAR
    scratch = [
        pltpu.VMEM(flat, bf16),
        pltpu.VMEM(flat, bf16),
        pltpu.VMEM(flat, bf16),
        pltpu.VMEM(flat, bf16),
        pltpu.VMEM((HEADS, 2, TOKENS, DIM), bf16),
        pltpu.VMEM((PATCH, DIM), bf16),
        pltpu.VMEM((HEADS, 2, TOKENS, DIM), bf16),
        pltpu.VMEM((HEADS, TOKENS, DIM), bf16),
        pltpu.VMEM((KEYS, DIM), bf16),
        pltpu.VMEM((KEYS, 2 * DIM), bf16),
        pltpu.VMEM((50, DIM), f32),
        pltpu.VMEM((PATCH, 1), f32),
        pltpu.VMEM((PATCH, 2 * DIM), f32),
        pltpu.VMEM((2, ROWS, DIM), bf16),
        pltpu.VMEM((2, ROWS, DIM), bf16),
        pltpu.VMEM((2, ROWS, DIM), bf16),
        pltpu.VMEM((2, ROWS, DIM), f32),
        pltpu.VMEM((2, 8, ROWS), f32),
        pltpu.VMEM((2, 8, ROWS), f32),
        pltpu.VMEM((2, ROWS, DIM), bf16),
        pltpu.VMEM(flat, bf16),
        pltpu.SMEM((1,), jnp.int32),
        pltpu.SMEM((1,), jnp.int32),
        pltpu.SMEM((1,), jnp.int32),
        dma((8,)),
        dma((2,)),
        dma,
        dma((2,)),
        dma((2,)),
        dma((2,)),
        dma,
        dma,
        dma,
        dma((2,)),
        dma((2,)),
        dma((2,)),
        dma((2,)),
        dma((2,)),
        dma((PLANES,)),
        dma((PLANES,)),
        dma,
        dma((PLANES,)),
        regular((PLANES,)),
        regular,
    ]
    anywhere = pl.BlockSpec(memory_space=pl.ANY)
    out = pl.pallas_call(
        kernel,
        out_shape=pltpu.VMEM(flat, bf16),
        in_specs=[anywhere] * 10,
        out_specs=pl.BlockSpec(memory_space=pltpu.VMEM),
        scratch_shapes=scratch,
        compiler_params=pltpu.CompilerParams(
            collective_id=0, has_side_effects=True, vmem_limit_bytes=56 * 2**20
        ),
        cost_estimate=pl.CostEstimate(
            flops=4 * PATCH * KEYS * DIM, bytes_accessed=2**22, transcendentals=PATCH * KEYS
        ),
    )(
        patch_index.reshape(1),
        text_lengths,
        timestep.reshape(1),
        hidden.reshape(flat),
        queries.reshape(flat),
        fresh_keys.reshape(flat),
        fresh_values.reshape(flat),
        stale_keys.reshape(STALE, DIM),
        stale_values.reshape(STALE, DIM),
        gate_table,
    )
    return out.reshape(1, 1, TOKENS, HEADS * DIM)


def solution(mesh):
    rows = P("cfg", "section", "seq", None)
    stale = P("cfg", "section", "seq", None, None)
    return jax.shard_map(
        body,
        mesh=mesh,
        in_specs=(
            rows, rows, rows, rows, stale, stale, P(None, "section", None), P(), P(), P("cfg"),
        ),
        out_specs=rows,
        check_vma=False,
    )
```
